32 devices in a mesh: groups: 2 (over x), ctx: 16 (over z, y, core).
Axes of the slice: x: 2, y: 2, z: 4, core: 2. Of those that a mesh axis runs over, the one named last changes fastest.
Arguments:
- q_span: bfloat16 [2048, 8192], P(('groups', 'ctx')), parts along dimension 0, may hold values from -200 to 200
- k_span: bfloat16 [2048, 1024], P(('groups', 'ctx')), parts along dimension 0, may hold values from -30 to 30
- v_span: bfloat16 [2048, 1024], P(('groups', 'ctx')), parts along dimension 0, may hold values from -6 to 6
- k_prefix: bfloat16 [1024, 1024], P(('groups', 'ctx')), parts along dimension 0, may hold values from -30 to 30
- v_prefix: bfloat16 [1024, 1024], P(('groups', 'ctx')), parts along dimension 0, may hold values from -6 to 6
- start_offset: int32 [2], P('groups'), parts along dimension 0, may hold values from 0 to 511
- prefix_len: int32 [2], P('groups'), parts along dimension 0, may hold values from 1 to 512
- block_order: int32 [64], P('groups'), parts along dimension 0, may hold values from 0 to 31, each once
Outputs:
- attended: bfloat16 [2048, 8192], P(('groups', 'ctx')), parts along dimension 0
The draws below stay inside these ranges and needn't reach their ends.
There are 2 independent parts, one for each index of `groups`. The reference program is written for one: setup_inputs(seed, part) draws one part's arguments, and reference() takes and returns one part's arrays. A program takes and returns all parts, laid end to end along the dimension named above; each array names one. Nothing has to cross between parts.
All inputs are finite; a program needn't handle non-finite values.
Results may differ from the reference program's by a relative error of at most 0.006.
Values may be sent and summed in bfloat16 or wider, within the bound.
A program may use at most 128 MiB of HBM per device.

```python
import math
import jax
import jax.numpy as jnp
from jax import lax

HQ = 64
KVH = 8
HD = 128
C_DEV = 64
SPAN = 1024
PREFIX = 512
N_CTX = 16


def draw_q_span(key, part):
    base = jnp.clip(jax.random.normal(jax.random.fold_in(key, 21), (SPAN, HQ * HD), jnp.float32), -6.0, 6.0)
    return base.astype(jnp.bfloat16)


def draw_k_span(key, part):
    base = jnp.clip(jax.random.normal(jax.random.fold_in(key, 22), (SPAN, KVH * HD), jnp.float32), -6.0, 6.0)
    return base.astype(jnp.bfloat16)


def draw_k_prefix(key, part):
    base = jnp.clip(jax.random.normal(jax.random.fold_in(key, 23), (PREFIX, KVH * HD), jnp.float32), -6.0, 6.0)
    return base.astype(jnp.bfloat16)


def levels(stream_key, extent, shards, low, high):
    def one(position, shards_of):
        steps = jax.random.uniform(jax.random.fold_in(jax.random.fold_in(stream_key, 6), position), (shards_of,), jnp.float32, low / len(shards), high / len(shards))
        return jnp.repeat(jnp.exp(steps), extent[position] // shards_of).reshape((-1,) + (1,) * (len(extent) - position - 1))

    gain = one(*shards[0])
    for cut in shards[1:]:
        gain = gain * one(*cut)
    return gain


def gaussian(own_key, dims, deviation, most, pieces=(), kind=jnp.bfloat16):
    level = levels(own_key, dims, pieces, -0.22, 0.18) if pieces else 1.0
    drawn = jax.random.normal(own_key, dims, jnp.float32) * deviation * level
    return jnp.minimum(jnp.maximum(drawn, -most), most).astype(kind)


def setup_inputs(seed: int = 0, part: int = 0) -> dict:
    key_list = jax.random.split(jax.random.key(seed), 9)
    own_keys = jax.random.split(jax.random.fold_in(key_list[8], part), 9)
    q_span = draw_q_span(jax.random.fold_in(jax.random.fold_in(key_list[8], part), 71), part)
    k_span = draw_k_span(jax.random.fold_in(jax.random.fold_in(key_list[8], part), 71), part)
    v_span = gaussian(own_keys[2], (SPAN, KVH * HD), 1.0, 6.0, ((0, 16),))
    k_prefix = draw_k_prefix(jax.random.fold_in(jax.random.fold_in(key_list[8], part), 71), part)
    v_prefix = gaussian(own_keys[4], (PREFIX, KVH * HD), 1.0, 6.0, ((0, 16),))
    start_offset = jax.random.randint(own_keys[5], (1,), 0, SPAN // 2).astype(jnp.int32)
    prefix_len = jax.random.randint(own_keys[6], (1,), 1, PREFIX + 1).astype(jnp.int32)
    block_order = jax.random.permutation(own_keys[7], 2 * N_CTX).astype(jnp.int32)
    return {"q_span": q_span, "k_span": k_span, "v_span": v_span, "k_prefix": k_prefix, "v_prefix": v_prefix, "start_offset": start_offset, "prefix_len": prefix_len, "block_order": block_order}


def reference(q_span, k_span, v_span, k_prefix, v_prefix, start_offset, prefix_len, block_order):
    total_rows = q_span.shape[0]
    block_rows = C_DEV // 2
    per_group = HQ // KVH
    row_ids = jnp.arange(total_rows, dtype=jnp.int32)
    positions = (block_order[row_ids // block_rows] * block_rows + row_ids % block_rows).astype(jnp.int32)
    prefix_ids = jnp.arange(k_prefix.shape[0], dtype=jnp.int32)
    prefix_ok = prefix_ids < prefix_len[0]
    key_all = jnp.concatenate([k_prefix, k_span], 0).astype(jnp.float32).reshape(-1, KVH, HD)
    value_all = jnp.concatenate([v_prefix, v_span], 0).astype(jnp.float32).reshape(-1, KVH, HD)
    scaling = 1.0 / math.sqrt(HD)
    query_block = math.gcd(total_rows, 128)
    count = total_rows // query_block
    query_blocks = q_span.reshape(count, query_block, KVH, per_group, HD)
    pos_blocks = positions.reshape(count, query_block)

    def one_block(packed):
        query_rows, query_pos = packed
        scores = jnp.einsum('qhgd,khd->hgqk', query_rows.astype(jnp.float32), key_all) * scaling
        causal = (positions[None, :] <= query_pos[:, None]) & (positions[None, :] >= start_offset[0])
        visible = jnp.concatenate([jnp.broadcast_to(prefix_ok[None, :], (query_block, prefix_ids.shape[0])), causal], 1)
        scores = jnp.where(visible[None, None], scores, jnp.float32(-1e+30))
        largest = lax.optimization_barrier(jnp.max(scores, axis=-1, keepdims=True))
        weights = jnp.where(visible[None, None], jnp.exp(scores - largest), jnp.float32(0.0))
        total = lax.optimization_barrier(jnp.sum(weights, axis=-1))
        rounded = lax.optimization_barrier(weights.astype(jnp.bfloat16)).astype(jnp.float32)
        summed = jnp.einsum('hgqk,khd->hgqd', rounded, value_all)
        result = summed / total[..., None]
        return result.transpose(2, 0, 1, 3).reshape(query_block, HQ * HD)
    outputs = lax.map(one_block, (query_blocks, pos_blocks))
    return outputs.reshape(total_rows, HQ * HD).astype(jnp.bfloat16)
```

```python
import functools
import math

import jax
import jax.numpy as jnp
from jax import lax
from jax.experimental import pallas as pl
from jax.experimental.pallas import tpu as pltpu
from jax.sharding import PartitionSpec as P

HD = 128
CORES = 2
NEG_FILL = -1e30
F32 = jnp.float32
BF16 = jnp.bfloat16


def kernel(chips, lanes, q_hbm, k_hbm, v_hbm, kp_hbm, vp_hbm, start_ref, plen_ref, order_ref,
           out_ref, buf, q_in, q_t, acc, top, tot, bias,
           in_sem, ring_send, ring_recv, sib_send, sib_recv):
    rows_span = k_hbm.shape[0]
    rows_pre = kp_hbm.shape[0]
    rows = rows_span + rows_pre
    block_rows = rows_span // 2
    heads_half = buf.shape[-1] // HD
    group = q_hbm.shape[1] // k_hbm.shape[1]
    width = group * rows_span
    rate = math.log2(math.e) / math.sqrt(HD)
    depth = chips // lanes

    me = lax.axis_index("ctx")
    chip, core = lax.div(me, CORES), lax.rem(me, CORES)
    other = 1 - core

    def chip_of(place):
        if lanes == 1:
            return place
        side = lax.div(place, depth)
        along = (1 - side) * place + side * (2 * depth - 1 - place)
        return along * 2 + side

    if lanes == 1:
        place = chip
    else:
        along, side = lax.div(chip, 2), lax.rem(chip, 2)
        place = (1 - side) * along + side * (2 * depth - 1 - along)
    after = chip_of(lax.rem(place + 1, chips)) * CORES + core
    before = chip_of(lax.rem(place + chips - 1, chips)) * CORES + core
    sibling = chip * CORES + other
    onward = (after, before)

    def origin(half, step):
        return lax.rem(place + (chips - step if half == 0 else step), chips)

    half_cols = buf.shape[-1]
    loads = []
    for kv, (span, pre) in enumerate(((k_hbm, kp_hbm), (v_hbm, vp_hbm))):
        for half in range(2):
            cols = pl.ds(half * half_cols, half_cols)
            for part, (src, at, size) in enumerate(((span, 0, rows_span), (pre, rows_span, rows_pre))):
                copy = pltpu.make_async_copy(
                    src.at[:, cols],
                    buf.at[half, place, kv, core, pl.ds(at, size)],
                    in_sem.at[kv * 4 + half * 2 + part],
                )
                copy.start()
                loads.append(copy)
    q_load = pltpu.make_async_copy(q_hbm, q_in, in_sem.at[8])
    q_load.start()

    barrier = pltpu.get_barrier_semaphore()
    for peer in (after, before, sibling):
        pl.semaphore_signal(barrier, inc=1, device_id={"ctx": peer}, device_id_type=pl.DeviceIdType.MESH)
    pl.semaphore_wait(barrier, 3)

    def ring(half, step, kv):
        piece = buf.at[half, origin(half, step), kv, core]
        return pltpu.make_async_remote_copy(
            src_ref=piece, dst_ref=piece,
            send_sem=ring_send.at[half, step, kv], recv_sem=ring_recv.at[half, step, kv],
            device_id={"ctx": onward[half]}, device_id_type=pl.DeviceIdType.MESH)

    def across(half, step, kv):
        piece = buf.at[half, origin(half, step), kv, core]
        return pltpu.make_async_remote_copy(
            src_ref=piece, dst_ref=piece,
            send_sem=sib_send.at[half, step, kv], recv_sem=sib_recv.at[half, step, kv],
            device_id={"ctx": sibling}, device_id_type=pl.DeviceIdType.MESH)

    def ring_arrival(half, step, kv):
        piece = buf.at[half, origin(half, step), kv, core]
        return pltpu.make_async_remote_copy(
            src_ref=piece, dst_ref=piece,
            send_sem=ring_send.at[half, step - 1, kv], recv_sem=ring_recv.at[half, step - 1, kv],
            device_id={"ctx": onward[half]}, device_id_type=pl.DeviceIdType.MESH)

    def across_arrival(half, step, kv):
        piece = buf.at[half, origin(half, step), kv, other]
        return pltpu.make_async_remote_copy(
            src_ref=piece, dst_ref=piece,
            send_sem=sib_send.at[half, step, kv], recv_sem=sib_recv.at[half, step, kv],
            device_id={"ctx": sibling}, device_id_type=pl.DeviceIdType.MESH)

    for kv in range(2):
        for half in range(2):
            for part in range(2):
                loads[kv * 4 + half * 2 + part].wait()
            ring(half, 0, kv).start()
    for kv in range(2):
        for half in range(2):
            across(half, 0, kv).start()

    q_load.wait()
    for head in range(2 * heads_half):
        stacked = jnp.concatenate(
            [q_in[:, (head * group + g) * HD:(head * group + g + 1) * HD] for g in range(group)], 0)
        q_t[head] = stacked.T
    acc[...] = jnp.zeros_like(acc)
    tot[...] = jnp.zeros_like(tot)
    top[...] = jnp.full_like(top, NEG_FILL)

    start = start_ref[0]
    plen = plen_ref[0]

    def positions(shape, device, axis):
        index = lax.broadcasted_iota(jnp.int32, shape, axis)
        if axis == 1:
            index = lax.rem(index, rows_span)
        first = order_ref[device * 2] * block_rows
        second = order_ref[device * 2 + 1] * block_rows
        return jnp.where(index < block_rows, first + index, second + index - block_rows)

    rep = 2 * rows_span
    q_pos = positions((1, rep), me, 1)

    def attend(half, step):
        for kv in range(2):
            across_arrival(half, step, kv).wait_recv()
        at = origin(half, step)
        source = chip_of(at)
        for c in range(CORES):
            device = source * CORES + c
            k_pos = positions((rows_span, rep), device, 0)
            seen = (k_pos <= q_pos) & (k_pos >= start)
            bias[c * rows:c * rows + rows_span] = jnp.where(seen, 0.0, NEG_FILL).astype(F32)
            slot = device * rows_pre + lax.broadcasted_iota(jnp.int32, (rows_pre, rep), 0)
            bias[c * rows + rows_span:(c + 1) * rows] = jnp.where(slot < plen, 0.0, NEG_FILL).astype(F32)
        shade = jnp.concatenate([bias[...]] * (width // rep), 1)
        for j in range(heads_half):
            head = half * heads_half + j
            cols = slice(j * HD, (j + 1) * HD)
            keys = buf[half, at, 0, :, :, cols].reshape(CORES * rows, HD)
            values = buf[half, at, 1, :, :, cols].reshape(CORES * rows, HD)
            score = jnp.dot(keys, q_t[head], preferred_element_type=F32) + shade
            old = top[head]
            new = jnp.maximum(old, jnp.max(score, axis=0, keepdims=True))
            shrink = jnp.exp2((old - new) * rate)
            weight = jnp.exp2((score - new) * rate)
            tot[head] = tot[head] * shrink + jnp.sum(weight, axis=0, keepdims=True)
            top[head] = new
            acc[head] = acc[head] * shrink + lax.dot_general(
                values, weight.astype(BF16), (((0,), (0,)), ((), ())), preferred_element_type=F32)

    def body(step, carry):
        for kv in range(2):
            for half in range(2):
                ring_arrival(half, step, kv).wait_recv()

                @pl.when(step < chips - 1)
                def _():
                    ring(half, step, kv).start()

                across(half, step, kv).start()
            attend(kv, step - 1)
        return carry

    lax.fori_loop(1, chips, body, 0)
    for half in range(2):
        attend(half, jnp.int32(chips - 1))

    for head in range(2 * heads_half):
        done = (acc[head] / tot[head]).T.astype(BF16)
        for g in range(group):
            out_ref[:, (head * group + g) * HD:(head * group + g + 1) * HD] = done[g * rows_span:(g + 1) * rows_span]

    def drain(step, carry):
        for kv in range(2):
            for half in range(2):
                across(half, step, kv).wait_send()

                @pl.when(step < chips - 1)
                def _():
                    ring(half, step, kv).wait_send()
        return carry

    lax.fori_loop(0, chips, drain, 0)


def local(chips, lanes, q_span, k_span, v_span, k_prefix, v_prefix, start_offset, prefix_len, block_order):
    rows_span, cols = k_span.shape
    rows = rows_span + k_prefix.shape[0]
    heads = cols // HD
    width = q_span.shape[1] // cols * rows_span
    steps = chips
    hbm = pl.BlockSpec(memory_space=pltpu.HBM)
    smem = pl.BlockSpec(memory_space=pltpu.SMEM)
    sems = pltpu.SemaphoreType.DMA((2, steps, 2))
    ops = heads * width * rows * CORES * chips
    return pl.pallas_call(
        functools.partial(kernel, chips, lanes),
        out_shape=jax.ShapeDtypeStruct(q_span.shape, BF16),
        in_specs=[hbm] * 5 + [smem] * 3,
        out_specs=pl.BlockSpec(memory_space=pltpu.VMEM),
        scratch_shapes=[
            pltpu.VMEM((2, chips, 2, CORES, rows, cols // 2), BF16),
            pltpu.VMEM(q_span.shape, BF16),
            pltpu.VMEM((heads, HD, width), BF16),
            pltpu.VMEM((heads, HD, width), F32),
            pltpu.VMEM((heads, 1, width), F32),
            pltpu.VMEM((heads, 1, width), F32),
            pltpu.VMEM((CORES * rows, 2 * rows_span), F32),
            pltpu.SemaphoreType.DMA((9,)),
            sems, sems, sems, sems,
        ],
        compiler_params=pltpu.CompilerParams(
            collective_id=0, has_side_effects=True, vmem_limit_bytes=48 * 1024 * 1024),
        cost_estimate=pl.CostEstimate(flops=4 * HD * ops, bytes_accessed=4 * q_span.size, transcendentals=ops),
    )(q_span, k_span, v_span, k_prefix, v_prefix, start_offset, prefix_len, block_order)


def solution(mesh):
    chips = mesh.shape["ctx"] // CORES
    lanes = 2 if mesh.shape["groups"] == 2 and chips % 2 == 0 else 1
    rows = P(("groups", "ctx"), None)
    one = P("groups")
    return jax.shard_map(
        functools.partial(local, chips, lanes), mesh=mesh,
        in_specs=(rows,) * 5 + (one,) * 3, out_specs=rows, check_vma=False
    )
```

```python
import functools
import math

import jax
import jax.numpy as jnp
from jax import lax
from jax.experimental import pallas as pl
from jax.experimental.pallas import tpu as pltpu
from jax.sharding import PartitionSpec as P

HD = 128
CORES = 2
NEG_FILL = -1e30
F32 = jnp.float32
BF16 = jnp.bfloat16


def kernel(chips, lanes, q_hbm, k_hbm, v_hbm, kp_hbm, vp_hbm, start_ref, plen_ref, order_ref,
           out_ref, buf, q_in, q_t, acc, top, tot, bias,
           in_sem, ring_send, ring_recv, sib_send, sib_recv):
    rows_span = k_hbm.shape[0]
    rows_pre = kp_hbm.shape[0]
    rows = rows_span + rows_pre
    block_rows = rows_span // 2
    heads_half = buf.shape[-1] // HD
    group = q_hbm.shape[1] // k_hbm.shape[1]
    width = group * rows_span
    rate = math.log2(math.e) / math.sqrt(HD)
    depth = chips // lanes

    me = lax.axis_index("ctx")
    chip, core = lax.div(me, CORES), lax.rem(me, CORES)
    other = 1 - core

    def chip_of(place):
        if lanes == 1:
            return place
        side = lax.div(place, depth)
        along = (1 - side) * place + side * (2 * depth - 1 - place)
        return along * 2 + side

    if lanes == 1:
        place = chip
    else:
        along, side = lax.div(chip, 2), lax.rem(chip, 2)
        place = (1 - side) * along + side * (2 * depth - 1 - along)
    after = chip_of(lax.rem(place + 1, chips)) * CORES + core
    before = chip_of(lax.rem(place + chips - 1, chips)) * CORES + core
    sibling = chip * CORES + other
    onward = (after, before)

    def origin(half, step):
        return lax.rem(place + (chips - step if half == 0 else step), chips)

    half_cols = buf.shape[-1]
    loads = []
    for kv, (span, pre) in enumerate(((k_hbm, kp_hbm), (v_hbm, vp_hbm))):
        for half in range(2):
            cols = pl.ds(half * half_cols, half_cols)
            for part, (src, at, size) in enumerate(((span, 0, rows_span), (pre, rows_span, rows_pre))):
                copy = pltpu.make_async_copy(
                    src.at[:, cols],
                    buf.at[half, place, kv, core, pl.ds(at, size)],
                    in_sem.at[kv * 4 + half * 2 + part],
                )
                copy.start()
                loads.append(copy)
    q_load = pltpu.make_async_copy(q_hbm, q_in, in_sem.at[8])
    q_load.start()

    barrier = pltpu.get_barrier_semaphore()
    for peer in (after, before, sibling):
        pl.semaphore_signal(barrier, inc=1, device_id={"ctx": peer}, device_id_type=pl.DeviceIdType.MESH)
    pl.semaphore_wait(barrier, 3)

    def ring(half, step, kv):
        piece = buf.at[half, origin(half, step), kv, core]
        return pltpu.make_async_remote_copy(
            src_ref=piece, dst_ref=piece,
            send_sem=ring_send.at[half, step, kv], recv_sem=ring_recv.at[half, step, kv],
            device_id={"ctx": onward[half]}, device_id_type=pl.DeviceIdType.MESH)

    def across(half, step, kv):
        piece = buf.at[half, origin(half, step), kv, core]
        return pltpu.make_async_remote_copy(
            src_ref=piece, dst_ref=piece,
            send_sem=sib_send.at[half, step, kv], recv_sem=sib_recv.at[half, step, kv],
            device_id={"ctx": sibling}, device_id_type=pl.DeviceIdType.MESH)

    def ring_arrival(half, step, kv):
        piece = buf.at[half, origin(half, step), kv, core]
        return pltpu.make_async_remote_copy(
            src_ref=piece, dst_ref=piece,
            send_sem=ring_send.at[half, step - 1, kv], recv_sem=ring_recv.at[half, step - 1, kv],
            device_id={"ctx": onward[half]}, device_id_type=pl.DeviceIdType.MESH)

    def across_arrival(half, step, kv):
        piece = buf.at[half, origin(half, step), kv, other]
        return pltpu.make_async_remote_copy(
            src_ref=piece, dst_ref=piece,
            send_sem=sib_send.at[half, step, kv], recv_sem=sib_recv.at[half, step, kv],
            device_id={"ctx": sibling}, device_id_type=pl.DeviceIdType.MESH)

    for kv in range(2):
        for half in range(2):
            for part in range(2):
                loads[kv * 4 + half * 2 + part].wait()
            ring(half, 0, kv).start()
    for kv in range(2):
        for half in range(2):
            across(half, 0, kv).start()

    q_load.wait()
    for head in range(2 * heads_half):
        stacked = jnp.concatenate(
            [q_in[:, (head * group + g) * HD:(head * group + g + 1) * HD] for g in range(group)], 0)
        q_t[head] = stacked.T
    acc[...] = jnp.zeros_like(acc)
    tot[...] = jnp.zeros_like(tot)
    top[...] = jnp.full_like(top, NEG_FILL)

    start = start_ref[0]
    plen = plen_ref[0]

    def positions(shape, device, axis):
        index = lax.broadcasted_iota(jnp.int32, shape, axis)
        if axis == 1:
            index = lax.rem(index, rows_span)
        first = order_ref[device * 2] * block_rows
        second = order_ref[device * 2 + 1] * block_rows
        return jnp.where(index < block_rows, first + index, second + index - block_rows)

    rep = 2 * rows_span
    q_pos = positions((1, rep), me, 1)

    def attend(half, step):
        for kv in range(2):
            across_arrival(half, step, kv).wait_recv()
        at = origin(half, step)
        source = chip_of(at)
        for c in range(CORES):
            device = source * CORES + c
            k_pos = positions((rows_span, rep), device, 0)
            seen = (k_pos <= q_pos) & (k_pos >= start)
            bias[c * rows:c * rows + rows_span] = jnp.where(seen, 0.0, NEG_FILL).astype(F32)
            slot = device * rows_pre + lax.broadcasted_iota(jnp.int32, (rows_pre, rep), 0)
            bias[c * rows + rows_span:(c + 1) * rows] = jnp.where(slot < plen, 0.0, NEG_FILL).astype(F32)
        shade = jnp.concatenate([bias[...]] * (width // rep), 1)
        for j in range(heads_half):
            head = half * heads_half + j
            cols = slice(j * HD, (j + 1) * HD)
            keys = buf[half, at, 0, :, :, cols].reshape(CORES * rows, HD)
            values = buf[half, at, 1, :, :, cols].reshape(CORES * rows, HD)
            score = jnp.dot(keys, q_t[head], preferred_element_type=F32) + shade
            old = top[head]
            new = jnp.maximum(old, jnp.max(score, axis=0, keepdims=True))
            shrink = jnp.exp2((old - new) * rate)
            weight = jnp.exp2((score - new) * rate)
            tot[head] = tot[head] * shrink + jnp.sum(weight, axis=0, keepdims=True)
            top[head] = new
            acc[head] = acc[head] * shrink + lax.dot_general(
                values, weight.astype(BF16), (((0,), (0,)), ((), ())), preferred_element_type=F32)

    def body(step, carry):
        for kv in range(2):
            for half in range(2):
                ring_arrival(half, step, kv).wait_recv()

                @pl.when(step < chips - 1)
                def _():
                    ring(half, step, kv).start()

                across(half, step, kv).start()
            attend(kv, step - 1)
        return carry

    lax.fori_loop(1, chips, body, 0)
    for half in range(2):
        attend(half, jnp.int32(chips - 1))

    for head in range(2 * heads_half):
        done = (acc[head] / tot[head]).T.astype(BF16)
        for g in range(group):
            out_ref[:, (head * group + g) * HD:(head * group + g + 1) * HD] = done[g * rows_span:(g + 1) * rows_span]

    def drain(step, carry):
        for kv in range(2):
            for half in range(2):
                across(half, step, kv).wait_send()

                @pl.when(step < chips - 1)
                def _():
                    ring(half, step, kv).wait_send()
        return carry

    lax.fori_loop(0, chips, drain, 0)


def local(chips, lanes, q_span, k_span, v_span, k_prefix, v_prefix, start_offset, prefix_len, block_order):
    rows_span, cols = k_span.shape
    rows = rows_span + k_prefix.shape[0]
    heads = cols // HD
    width = q_span.shape[1] // cols * rows_span
    steps = chips
    hbm = pl.BlockSpec(memory_space=pltpu.HBM)
    smem = pl.BlockSpec(memory_space=pltpu.SMEM)
    sems = pltpu.SemaphoreType.DMA((2, steps, 2))
    ops = heads * width * rows * CORES * chips
    return pl.pallas_call(
        functools.partial(kernel, chips, lanes),
        out_shape=jax.ShapeDtypeStruct(q_span.shape, BF16),
        in_specs=[hbm] * 5 + [smem] * 3,
        out_specs=pl.BlockSpec(memory_space=pltpu.VMEM),
        scratch_shapes=[
            pltpu.VMEM((2, chips, 2, CORES, rows, cols // 2), BF16),
            pltpu.VMEM(q_span.shape, BF16),
            pltpu.VMEM((heads, HD, width), BF16),
            pltpu.VMEM((heads, HD, width), F32),
            pltpu.VMEM((heads, 1, width), F32),
            pltpu.VMEM((heads, 1, width), F32),
            pltpu.VMEM((CORES * rows, 2 * rows_span), F32),
            pltpu.SemaphoreType.DMA((9,)),
            sems, sems, sems, sems,
        ],
        compiler_params=pltpu.CompilerParams(
            collective_id=0, has_side_effects=True, vmem_limit_bytes=63 * 1024 * 1024),
        cost_estimate=pl.CostEstimate(flops=4 * HD * ops, bytes_accessed=4 * q_span.size, transcendentals=ops),
    )(q_span, k_span, v_span, k_prefix, v_prefix, start_offset, prefix_len, block_order)


def solution(mesh):
    chips = mesh.shape["ctx"] // CORES
    lanes = 2 if mesh.shape["groups"] == 2 and chips % 2 == 0 else 1
    rows = P(("groups", "ctx"), None)
    one = P("groups")
    return jax.shard_map(
        functools.partial(local, chips, lanes), mesh=mesh,
        in_specs=(rows,) * 5 + (one,) * 3, out_specs=rows, check_vma=False
    )
```

```python
import functools
import math

import jax
import jax.numpy as jnp
from jax import lax
from jax.experimental import pallas as pl
from jax.experimental.pallas import tpu as pltpu
from jax.sharding import PartitionSpec as P

HD = 128
CORES = 2
NEG_FILL = -1e30
F32 = jnp.float32
BF16 = jnp.bfloat16


def kernel(chips, lanes, q_hbm, k_hbm, v_hbm, kp_hbm, vp_hbm, start_ref, plen_ref, order_ref,
           out_ref, buf, q_in, q_t, acc, top, tot, bias,
           in_sem, ring_send, ring_recv, sib_send, sib_recv):
    rows_span = k_hbm.shape[0]
    rows_pre = kp_hbm.shape[0]
    rows = rows_span + rows_pre
    block_rows = rows_span // 2
    heads_half = buf.shape[-1] // HD
    group = q_hbm.shape[1] // k_hbm.shape[1]
    width = group * rows_span
    rate = math.log2(math.e) / math.sqrt(HD)
    depth = chips // lanes

    me = lax.axis_index("ctx")
    chip, core = lax.div(me, CORES), lax.rem(me, CORES)
    other = 1 - core

    def chip_of(place):
        if lanes == 1:
            return place
        side = lax.div(place, depth)
        along = (1 - side) * place + side * (2 * depth - 1 - place)
        return along * 2 + side

    if lanes == 1:
        place = chip
    else:
        along, side = lax.div(chip, 2), lax.rem(chip, 2)
        place = (1 - side) * along + side * (2 * depth - 1 - along)
    after = chip_of(lax.rem(place + 1, chips)) * CORES + core
    before = chip_of(lax.rem(place + chips - 1, chips)) * CORES + core
    sibling = chip * CORES + other
    onward = (after, before)

    def origin(way, step):
        return lax.rem(place + (chips - step if way == 0 else step), chips)

    def piece(way, step, turn, holder):
        half = way if turn < 2 else 1 - way
        return buf.at[half, origin(way, step), turn % 2, holder]

    half_cols = buf.shape[-1]
    loads = []
    for kv, (span, pre) in enumerate(((k_hbm, kp_hbm), (v_hbm, vp_hbm))):
        for half in range(2):
            cols = pl.ds(half * half_cols, half_cols)
            for part, (src, at, size) in enumerate(((span, 0, rows_span), (pre, rows_span, rows_pre))):
                copy = pltpu.make_async_copy(
                    src.at[:, cols],
                    buf.at[half, place, kv, core, pl.ds(at, size)],
                    in_sem.at[kv * 4 + half * 2 + part],
                )
                copy.start()
                loads.append(copy)
    q_load = pltpu.make_async_copy(q_hbm, q_in, in_sem.at[8])
    q_load.start()

    barrier = pltpu.get_barrier_semaphore()
    for peer in (after, before, sibling):
        pl.semaphore_signal(barrier, inc=1, device_id={"ctx": peer}, device_id_type=pl.DeviceIdType.MESH)
    pl.semaphore_wait(barrier, 3)

    def move(ref, step, way, turn, sends, recvs, peer):
        return pltpu.make_async_remote_copy(
            src_ref=ref, dst_ref=ref,
            send_sem=sends.at[way, step, turn], recv_sem=recvs.at[way, step, turn],
            device_id={"ctx": peer}, device_id_type=pl.DeviceIdType.MESH)

    def ring(way, step, turn):
        return move(piece(way, step, turn, core), step, way, turn, ring_send, ring_recv, onward[way])

    def ring_arrival(way, step, turn):
        return move(piece(way, step, turn, core), step - 1, way, turn, ring_send, ring_recv, onward[way])

    def across(way, step, turn):
        return move(piece(way, step, turn, core), step, way, turn, sib_send, sib_recv, sibling)

    def across_arrival(way, step, turn):
        return move(piece(way, step, turn, other), step, way, turn, sib_send, sib_recv, sibling)

    for turn in range(4):
        for way in range(2):
            half = way if turn < 2 else 1 - way
            if turn < 2:
                for part in range(2):
                    loads[turn * 4 + half * 2 + part].wait()
            ring(way, 0, turn).start()
    for turn in (2, 3):
        for way in range(2):
            across(way, 0, turn).start()

    q_load.wait()
    for head in range(2 * heads_half):
        stacked = jnp.concatenate(
            [q_in[:, (head * group + g) * HD:(head * group + g + 1) * HD] for g in range(group)], 0)
        q_t[head] = stacked.T
    acc[...] = jnp.zeros_like(acc)
    tot[...] = jnp.zeros_like(tot)
    top[...] = jnp.full_like(top, NEG_FILL)

    start = start_ref[0]
    plen = plen_ref[0]

    def positions(shape, device, axis):
        index = lax.broadcasted_iota(jnp.int32, shape, axis)
        if axis == 1:
            index = lax.rem(index, rows_span)
        first = order_ref[device * 2] * block_rows
        second = order_ref[device * 2 + 1] * block_rows
        return jnp.where(index < block_rows, first + index, second + index - block_rows)

    rep = 2 * rows_span
    q_pos = positions((1, rep), me, 1)

    def attend(way, step, late, last=False):
        half = 1 - way if late else way
        for kv in range(2):
            across_arrival(way, step, 2 * late + kv).wait_recv()
        at = origin(way, step)
        source = chip_of(at)
        for c in range(CORES):
            device = source * CORES + c
            k_pos = positions((rows_span, rep), device, 0)
            seen = (k_pos <= q_pos) & (k_pos >= start)
            bias[c * rows:c * rows + rows_span] = jnp.where(seen, 0.0, NEG_FILL).astype(F32)
            slot = device * rows_pre + lax.broadcasted_iota(jnp.int32, (rows_pre, rep), 0)
            bias[c * rows + rows_span:(c + 1) * rows] = jnp.where(slot < plen, 0.0, NEG_FILL).astype(F32)
        shade = jnp.concatenate([bias[...]] * (width // rep), 1)
        for j in range(heads_half):
            head = half * heads_half + j
            cols = slice(j * HD, (j + 1) * HD)
            keys = buf[half, at, 0, :, :, cols].reshape(CORES * rows, HD)
            values = buf[half, at, 1, :, :, cols].reshape(CORES * rows, HD)
            score = jnp.dot(keys, q_t[head], preferred_element_type=F32) + shade
            old = top[head]
            new = jnp.maximum(old, jnp.max(score, axis=0, keepdims=True))
            shrink = jnp.exp2((old - new) * rate)
            weight = jnp.exp2((score - new) * rate)
            total = tot[head] * shrink + jnp.sum(weight, axis=0, keepdims=True)
            summed = acc[head] * shrink + lax.dot_general(
                values, weight.astype(BF16), (((0,), (0,)), ((), ())), preferred_element_type=F32)
            if last:
                done = (summed * (1.0 / total)).T.astype(BF16)
                for g in range(group):
                    out_ref[:, (head * group + g) * HD:(head * group + g + 1) * HD] = (
                        done[g * rows_span:(g + 1) * rows_span])
            else:
                tot[head] = total
                top[head] = new
                acc[head] = summed

    hops = chips // 2

    def body(step, carry):
        for turn in range(4):
            for way in range(2):
                ring_arrival(way, step, turn).wait_recv()
                if turn < 2:
                    ring(way, step, turn).start()
                else:
                    @pl.when(step < hops - 1)
                    def _():
                        ring(way, step, turn).start()

                across(way, step, turn).start()
            if turn < 2:
                attend(turn, step - 1, 1)
            else:
                attend(turn - 2, step, 0)
        return carry

    lax.fori_loop(1, hops, body, 0)
    end = jnp.int32(hops)
    for turn in range(2):
        for way in range(2):
            ring_arrival(way, end, turn).wait_recv()
            across(way, end, turn).start()
        attend(turn, end - 1, 1)
    for way in range(2):
        attend(way, end, 0, True)

    def drain(step, carry):
        for turn in range(4):
            for way in range(2):
                if turn < 2:
                    ring(way, step, turn).wait_send()

                    @pl.when(step > 0)
                    def _():
                        across(way, step, turn).wait_send()
                else:
                    across(way, step, turn).wait_send()

                    @pl.when(step < hops - 1)
                    def _():
                        ring(way, step, turn).wait_send()
        return carry

    lax.fori_loop(0, hops, drain, 0)
    for turn in range(2):
        for way in range(2):
            across(way, end, turn).wait_send()


def local(chips, lanes, q_span, k_span, v_span, k_prefix, v_prefix, start_offset, prefix_len, block_order):
    rows_span, cols = k_span.shape
    rows = rows_span + k_prefix.shape[0]
    heads = cols // HD
    width = q_span.shape[1] // cols * rows_span
    steps = chips // 2 + 1
    hbm = pl.BlockSpec(memory_space=pltpu.HBM)
    smem = pl.BlockSpec(memory_space=pltpu.SMEM)
    sems = pltpu.SemaphoreType.DMA((2, steps, 4))
    ops = heads * width * rows * CORES * chips
    return pl.pallas_call(
        functools.partial(kernel, chips, lanes),
        out_shape=jax.ShapeDtypeStruct(q_span.shape, BF16),
        in_specs=[hbm] * 5 + [smem] * 3,
        out_specs=pl.BlockSpec(memory_space=pltpu.VMEM),
        scratch_shapes=[
            pltpu.VMEM((2, chips, 2, CORES, rows, cols // 2), BF16),
            pltpu.VMEM(q_span.shape, BF16),
            pltpu.VMEM((heads, HD, width), BF16),
            pltpu.VMEM((heads, HD, width), F32),
            pltpu.VMEM((heads, 1, width), F32),
            pltpu.VMEM((heads, 1, width), F32),
            pltpu.VMEM((CORES * rows, 2 * rows_span), F32),
            pltpu.SemaphoreType.DMA((9,)),
            sems, sems, sems, sems,
        ],
        compiler_params=pltpu.CompilerParams(
            collective_id=0, has_side_effects=True, vmem_limit_bytes=63 * 1024 * 1024),
        cost_estimate=pl.CostEstimate(flops=4 * HD * ops, bytes_accessed=4 * q_span.size, transcendentals=ops),
    )(q_span, k_span, v_span, k_prefix, v_prefix, start_offset, prefix_len, block_order)


def solution(mesh):
    chips = mesh.shape["ctx"] // CORES
    lanes = 2 if mesh.shape["groups"] == 2 and chips % 2 == 0 else 1
    rows = P(("groups", "ctx"), None)
    one = P("groups")
    return jax.shard_map(
        functools.partial(local, chips, lanes), mesh=mesh,
        in_specs=(rows,) * 5 + (one,) * 3, out_specs=rows, check_vma=False
    )
```

```python
import functools
import math

import jax
import jax.numpy as jnp
from jax import lax
from jax.experimental import pallas as pl
from jax.experimental.pallas import tpu as pltpu
from jax.sharding import PartitionSpec as P

HD = 128
CORES = 2
NEG_FILL = -1e30
F32 = jnp.float32
BF16 = jnp.bfloat16


def kernel(chips, lanes, q_hbm, k_hbm, v_hbm, kp_hbm, vp_hbm, start_hbm, plen_hbm, order_hbm,
           out_hbm, start_ref, plen_ref, order_ref, out_ref, buf, q_in, q_t, acc, top, tot, bias,
           in_sem, num_sem, out_sem, ring_send, ring_recv, sib_send, sib_recv):
    rows_span = k_hbm.shape[0]
    rows_pre = kp_hbm.shape[0]
    rows = rows_span + rows_pre
    block_rows = rows_span // 2
    heads_half = buf.shape[-1] // HD
    group = q_hbm.shape[1] // k_hbm.shape[1]
    width = group * rows_span
    rate = math.log2(math.e) / math.sqrt(HD)
    depth = chips // lanes

    me = lax.axis_index("ctx")
    chip, core = lax.div(me, CORES), lax.rem(me, CORES)
    other = 1 - core

    def chip_of(place):
        if lanes == 1:
            return place
        side = lax.div(place, depth)
        along = (1 - side) * place + side * (2 * depth - 1 - place)
        return along * 2 + side

    if lanes == 1:
        place = chip
    else:
        along, side = lax.div(chip, 2), lax.rem(chip, 2)
        place = (1 - side) * along + side * (2 * depth - 1 - along)
    after = chip_of(lax.rem(place + 1, chips)) * CORES + core
    before = chip_of(lax.rem(place + chips - 1, chips)) * CORES + core
    sibling = chip * CORES + other
    onward = (after, before)

    def origin(way, step):
        return lax.rem(place + (chips - step if way == 0 else step), chips)

    def piece(way, step, turn, holder):
        half = way if turn < 2 else 1 - way
        return buf.at[half, origin(way, step), turn % 2, holder]

    barrier = pltpu.get_barrier_semaphore()
    for peer in (after, before, sibling):
        pl.semaphore_signal(barrier, inc=1, device_id={"ctx": peer}, device_id_type=pl.DeviceIdType.MESH)

    half_cols = buf.shape[-1]
    loads = []
    for kv, (span, pre) in enumerate(((k_hbm, kp_hbm), (v_hbm, vp_hbm))):
        for half in range(2):
            cols = pl.ds(half * half_cols, half_cols)
            for part, (src, at, size) in enumerate(((span, 0, rows_span), (pre, rows_span, rows_pre))):
                copy = pltpu.make_async_copy(
                    src.at[:, cols],
                    buf.at[half, place, kv, core, pl.ds(at, size)],
                    in_sem.at[kv * 4 + half * 2 + part],
                )
                copy.start()
                loads.append(copy)
    q_load = pltpu.make_async_copy(q_hbm, q_in, in_sem.at[8])
    q_load.start()

    numbers = [
        pltpu.make_async_copy(src, dst, num_sem.at[i])
        for i, (src, dst) in enumerate(((start_hbm, start_ref), (plen_hbm, plen_ref), (order_hbm, order_ref)))
    ]
    for copy in numbers:
        copy.start()
    pl.semaphore_wait(barrier, 3)

    def move(ref, step, way, turn, sends, recvs, peer):
        return pltpu.make_async_remote_copy(
            src_ref=ref, dst_ref=ref,
            send_sem=sends.at[way, step, turn], recv_sem=recvs.at[way, step, turn],
            device_id={"ctx": peer}, device_id_type=pl.DeviceIdType.MESH)

    def ring(way, step, turn):
        return move(piece(way, step, turn, core), step, way, turn, ring_send, ring_recv, onward[way])

    def ring_arrival(way, step, turn):
        return move(piece(way, step, turn, core), step - 1, way, turn, ring_send, ring_recv, onward[way])

    def across(way, step, turn):
        return move(piece(way, step, turn, core), step, way, turn, sib_send, sib_recv, sibling)

    def across_arrival(way, step, turn):
        return move(piece(way, step, turn, other), step, way, turn, sib_send, sib_recv, sibling)

    for turn in range(4):
        for way in range(2):
            half = way if turn < 2 else 1 - way
            if turn < 2:
                for part in range(2):
                    loads[turn * 4 + half * 2 + part].wait()
            ring(way, 0, turn).start()
    for turn in (2, 3):
        for way in range(2):
            across(way, 0, turn).start()

    q_load.wait()
    for head in range(2 * heads_half):
        stacked = jnp.concatenate(
            [q_in[:, (head * group + g) * HD:(head * group + g + 1) * HD] for g in range(group)], 0)
        q_t[head] = stacked.T
    acc[...] = jnp.zeros_like(acc)
    tot[...] = jnp.zeros_like(tot)
    top[...] = jnp.full_like(top, NEG_FILL)

    for copy in numbers:
        copy.wait()
    start = start_ref[0]
    plen = plen_ref[0]

    def positions(shape, device, axis):
        index = lax.broadcasted_iota(jnp.int32, shape, axis)
        if axis == 1:
            index = lax.rem(index, rows_span)
        first = order_ref[device * 2] * block_rows
        second = order_ref[device * 2 + 1] * block_rows
        return jnp.where(index < block_rows, first + index, second + index - block_rows)

    rep = 2 * rows_span
    q_pos = positions((1, rep), me, 1)

    def store(head):
        cols = pl.ds(head * group * HD, group * HD)
        return pltpu.make_async_copy(out_ref.at[:, cols], out_hbm.at[:, cols], out_sem.at[head])

    def attend(way, step, late, last=False):
        half = 1 - way if late else way
        for kv in range(2):
            across_arrival(way, step, 2 * late + kv).wait_recv()
        at = origin(way, step)
        source = chip_of(at)
        for c in range(CORES):
            device = source * CORES + c
            k_pos = positions((rows_span, rep), device, 0)
            seen = (k_pos <= q_pos) & (k_pos >= start)
            bias[c * rows:c * rows + rows_span] = jnp.where(seen, 0.0, NEG_FILL).astype(F32)
            slot = device * rows_pre + lax.broadcasted_iota(jnp.int32, (rows_pre, rep), 0)
            bias[c * rows + rows_span:(c + 1) * rows] = jnp.where(slot < plen, 0.0, NEG_FILL).astype(F32)
        shade = jnp.concatenate([bias[...]] * (width // rep), 1)
        for j in range(heads_half):
            head = half * heads_half + j
            cols = slice(j * HD, (j + 1) * HD)
            keys = buf[half, at, 0, :, :, cols].reshape(CORES * rows, HD)
            values = buf[half, at, 1, :, :, cols].reshape(CORES * rows, HD)
            score = jnp.dot(keys, q_t[head], preferred_element_type=F32) + shade
            old = top[head]
            new = jnp.maximum(old, jnp.max(score, axis=0, keepdims=True))
            shrink = jnp.exp2((old - new) * rate)
            weight = jnp.exp2((score - new) * rate)
            total = tot[head] * shrink + jnp.sum(weight, axis=0, keepdims=True)
            summed = acc[head] * shrink + lax.dot_general(
                values, weight.astype(BF16), (((0,), (0,)), ((), ())), preferred_element_type=F32)
            if last:
                done = (summed * (1.0 / total)).T.astype(BF16)
                for g in range(group):
                    out_ref[:, (head * group + g) * HD:(head * group + g + 1) * HD] = (
                        done[g * rows_span:(g + 1) * rows_span])
                store(head).start()
            else:
                tot[head] = total
                top[head] = new
                acc[head] = summed

    hops = chips // 2

    def body(step, carry):
        for turn in range(4):
            for way in range(2):
                ring_arrival(way, step, turn).wait_recv()
                if turn < 2:
                    ring(way, step, turn).start()
                else:
                    @pl.when(step < hops - 1)
                    def _():
                        ring(way, step, turn).start()

                across(way, step, turn).start()
            if turn < 2:
                attend(turn, step - 1, 1)
            else:
                attend(turn - 2, step, 0)
        return carry

    lax.fori_loop(1, hops, body, 0)
    end = jnp.int32(hops)
    for turn in range(2):
        for way in range(2):
            ring_arrival(way, end, turn).wait_recv()
            across(way, end, turn).start()
        attend(turn, end - 1, 1)
    for way in range(2):
        attend(way, end, 0, True)

    def drain(step, carry):
        for turn in range(4):
            for way in range(2):
                if turn < 2:
                    ring(way, step, turn).wait_send()

                    @pl.when(step > 0)
                    def _():
                        across(way, step, turn).wait_send()
                else:
                    across(way, step, turn).wait_send()

                    @pl.when(step < hops - 1)
                    def _():
                        ring(way, step, turn).wait_send()
        return carry

    lax.fori_loop(0, hops, drain, 0)
    for turn in range(2):
        for way in range(2):
            across(way, end, turn).wait_send()
    for head in range(2 * heads_half):
        store(head).wait()


def local(chips, lanes, q_span, k_span, v_span, k_prefix, v_prefix, start_offset, prefix_len, block_order):
    rows_span, cols = k_span.shape
    rows = rows_span + k_prefix.shape[0]
    heads = cols // HD
    width = q_span.shape[1] // cols * rows_span
    steps = chips // 2 + 1
    hbm = pl.BlockSpec(memory_space=pltpu.HBM)
    sems = pltpu.SemaphoreType.DMA((2, steps, 4))
    ops = heads * width * rows * CORES * chips
    return pl.pallas_call(
        functools.partial(kernel, chips, lanes),
        out_shape=jax.ShapeDtypeStruct(q_span.shape, BF16),
        in_specs=[hbm] * 8,
        out_specs=hbm,
        scratch_shapes=[
            pltpu.SMEM(start_offset.shape, jnp.int32),
            pltpu.SMEM(prefix_len.shape, jnp.int32),
            pltpu.SMEM(block_order.shape, jnp.int32),
            pltpu.VMEM(q_span.shape, BF16),
            pltpu.VMEM((2, chips, 2, CORES, rows, cols // 2), BF16),
            pltpu.VMEM(q_span.shape, BF16),
            pltpu.VMEM((heads, HD, width), BF16),
            pltpu.VMEM((heads, HD, width), F32),
            pltpu.VMEM((heads, 1, width), F32),
            pltpu.VMEM((heads, 1, width), F32),
            pltpu.VMEM((CORES * rows, 2 * rows_span), F32),
            pltpu.SemaphoreType.DMA((9,)),
            pltpu.SemaphoreType.DMA((3,)),
            pltpu.SemaphoreType.DMA((heads,)),
            sems, sems, sems, sems,
        ],
        compiler_params=pltpu.CompilerParams(
            collective_id=0, has_side_effects=True, vmem_limit_bytes=63 * 1024 * 1024),
        cost_estimate=pl.CostEstimate(flops=4 * HD * ops, bytes_accessed=4 * q_span.size, transcendentals=ops),
    )(q_span, k_span, v_span, k_prefix, v_prefix, start_offset, prefix_len, block_order)


def solution(mesh):
    chips = mesh.shape["ctx"] // CORES
    lanes = 2 if mesh.shape["groups"] == 2 and chips % 2 == 0 else 1
    rows = P(("groups", "ctx"), None)
    one = P("groups")
    return jax.shard_map(
        functools.partial(local, chips, lanes), mesh=mesh,
        in_specs=(rows,) * 5 + (one,) * 3, out_specs=rows, check_vma=False
    )
```
